256 devices in a mesh: cells: 32 (over y, x, core), genes: 8 (over z).
Axes of the slice: x: 4, y: 4, z: 8, core: 2. Of those that a mesh axis runs over, the one named last changes fastest.
Arguments:
- theta_shape: float32 [65536, 128], P(('cells', 'genes')), may hold values from 0.5 to 5
- theta_rate: float32 [65536, 128], P(('cells', 'genes')), may hold values from 8192 to 131072
- cell_activity: float32 [65536], P(('cells', 'genes')), may hold values from 1 to 10
- beta_shape: float32 [32768, 128], P(('cells', 'genes')), may hold values from 0.5 to 5
- beta_rate: float32 [32768, 128], P(('cells', 'genes')), may hold values from 4096 to 65536
- gene_activity: float32 [32768], P(('cells', 'genes')), may hold values from 1 to 10
- block_ids: int32 [8, 32, 16], P('genes', 'cells'), may hold values from 0 to 31, as said below
- live_blocks: int32 [8, 32], P('genes', 'cells'), may hold values from 2 to 16, as said below
- counts: bfloat16 [8, 16, 65536, 128], P('genes', None, 'cells'), may hold values from 0 to 15, as said below
Outputs:
- log_theta_shape: float32 [65536, 128], P(('cells', 'genes'))
- log_theta_rate: float32 [65536, 128], P(('cells', 'genes'))
- log_beta_shape: float32 [32768, 128], P(('cells', 'genes'))
- log_beta_rate: float32 [32768, 128], P(('cells', 'genes'))
The draws below stay inside these ranges and needn't reach their ends.
Inputs may be any that keep to these rules, and one draw needn't show every extreme that they name: `block_ids`: the 16 block numbers of one cell shard in one gene group are distinct. `live_blocks`: some cell shard in some gene group has all 16 slots live in every draw. `counts`: Non-negative whole numbers; tiles of slots that are not live hold numbers too and do not count.
All inputs are finite; a program needn't handle non-finite values.
Results may differ from the reference program's by a relative error of at most 0.00074.
Values may be sent and summed in bfloat16 or wider, within the bound.
No kernel may reach another device: no remote copies, remote signals or barrier semaphores. Data moves between devices by JAX's collectives and lax.ppermute only.
A program may use at most 64 MiB of HBM per device.

```python
import math
import jax
import jax.numpy as jnp
from jax import lax

K = 128
G = 32768
BLOCK = 128
C_DEV = 2048
SLOTS = 16
GROUPS = 8
SHARDS = 32
CELLS = 65536
OWN = 128
GROUP_GENES = 4096
GROUP_BLOCKS = 32


def draw_block_ids(key, part):
    key = jax.random.fold_in(key, 11)
    key_list = jax.random.split(key, GROUPS * SHARDS)

    def one_list(one_key):
        return jax.random.permutation(one_key, GROUP_BLOCKS)[:SLOTS].astype(jnp.int32)
    return jax.vmap(one_list)(key_list).reshape(GROUPS, SHARDS, SLOTS)


def draw_live_blocks(key, part):
    key = jax.random.fold_in(key, 23)
    first, second, third = jax.random.split(key, 3)
    total = GROUPS * SHARDS
    base_count = jax.random.randint(first, (total,), 2, SLOTS // 2 + 1)
    full_mark = jax.random.randint(second, (total,), 0, 8) == 0
    live_count = jnp.where(full_mark, SLOTS, base_count)
    chosen = jax.random.randint(third, (), 0, total)
    live_count = jnp.where(jnp.arange(total) == chosen, SLOTS, live_count)
    return live_count.reshape(GROUPS, SHARDS).astype(jnp.int32)


def draw_counts(key, part):
    key = jax.random.fold_in(key, 37)
    first, second = jax.random.split(key, 2)
    depth = jax.random.randint(first, (1, 1, CELLS, 1), 2, 17)
    raw_value = jax.random.randint(second, (GROUPS, SLOTS, CELLS, BLOCK), 0, 40)
    value = jnp.where(raw_value < 16, jnp.remainder(raw_value, depth), 0)
    return value.astype(jnp.float32).astype(jnp.bfloat16)


def levels(stream_key, extent, pieces, smallest, high):
    level, own = 1.0, jax.random.fold_in(stream_key, 6)
    for dim, blocks in pieces:
        draws = jnp.exp(jax.random.uniform(jax.random.fold_in(own, dim), (blocks,), jnp.float32, smallest / len(pieces), high / len(pieces)))
        level = level * jnp.repeat(draws, extent[dim] // blocks).reshape([-1 if axis == dim else 1 for axis in range(len(extent))])
    return level


def setup_inputs(seed: int = 0) -> dict:
    key_of = jax.random.split(jax.random.key(seed), 10)
    theta_shape = jnp.clip(jnp.exp(math.log(5.0) - 2.3025851 * jax.random.uniform(key_of[0], (CELLS, K), jnp.float32) ** levels(key_of[0], (CELLS, K), ((0, 256),), -0.2, 0.2)), 0.5, 5.0)
    theta_rate = jnp.clip(jnp.exp(math.log(131072.0) - 2.7725887 * jax.random.uniform(key_of[1], (CELLS, K), jnp.float32) ** levels(key_of[1], (CELLS, K), ((0, 256),), -0.2, 0.2)), 8192.0, 131072.0)
    cell_activity = jnp.clip(jnp.exp(math.log(10.0) - 2.3025851 * jax.random.uniform(key_of[2], (CELLS,), jnp.float32) ** levels(key_of[2], (CELLS,), ((0, 256),), -0.2, 0.2)), 1.0, 10.0)
    beta_shape = jnp.clip(jnp.exp(math.log(5.0) - 2.3025851 * jax.random.uniform(key_of[3], (G, K), jnp.float32) ** levels(key_of[3], (G, K), ((0, 256),), -0.2, 0.2)), 0.5, 5.0)
    beta_rate = jnp.clip(jnp.exp(math.log(65536.0) - 2.7725887 * jax.random.uniform(key_of[4], (G, K), jnp.float32) ** levels(key_of[4], (G, K), ((0, 256),), -0.2, 0.2)), 4096.0, 65536.0)
    gene_activity = jnp.clip(jnp.exp(math.log(10.0) - 2.3025851 * jax.random.uniform(key_of[5], (G,), jnp.float32) ** levels(key_of[5], (G,), ((0, 256),), -0.2, 0.2)), 1.0, 10.0)
    block_ids = draw_block_ids(jax.random.fold_in(key_of[9], 71), 0)
    live_blocks = draw_live_blocks(jax.random.fold_in(key_of[9], 71), 0)
    counts = draw_counts(jax.random.fold_in(key_of[9], 71), 0)
    return {"theta_shape": theta_shape, "theta_rate": theta_rate, "cell_activity": cell_activity, "beta_shape": beta_shape, "beta_rate": beta_rate, "gene_activity": gene_activity, "block_ids": block_ids, "live_blocks": live_blocks, "counts": counts}


def digamma_series(value):
    shifted = value
    correction = jnp.zeros_like(value)
    for offset in range(6):
        correction = correction + 1.0 / shifted
        shifted = shifted + 1.0
    inverse = 1.0 / shifted
    square = inverse * inverse
    series = jnp.log(shifted) - 0.5 * inverse - square * (1.0 / 12.0 - square * (1.0 / 120.0 - square * (1.0 / 252.0)))
    return series - correction


def reference(theta_shape, theta_rate, cell_activity, beta_shape, beta_rate, gene_activity, block_ids, live_blocks, counts):
    theta_total = jnp.sum(theta_shape / theta_rate, axis=0)
    beta_total = jnp.sum(beta_shape / beta_rate, axis=0)
    theta_weight = jnp.exp(digamma_series(theta_shape) - jnp.log(theta_rate)).astype(jnp.bfloat16)
    beta_weight = jnp.exp(digamma_series(beta_shape) - jnp.log(beta_rate)).astype(jnp.bfloat16)
    group_view = beta_weight.reshape(SHARDS, GROUPS, OWN, K)
    cell_stat = jnp.zeros((CELLS, K), jnp.float32)
    gene_parts = []
    for group_index in range(GROUPS):
        group_weight = group_view[:, group_index].reshape(GROUP_GENES, K)
        group_counts = counts[group_index]
        group_ids = block_ids[group_index]
        group_live = live_blocks[group_index]

        def per_shard(gene_acc, shard_index):
            cell_rows = lax.dynamic_slice_in_dim(theta_weight, shard_index * C_DEV, C_DEV, 0)
            count_tiles = lax.dynamic_slice_in_dim(group_counts, shard_index * C_DEV, C_DEV, 1)
            slot_ids = group_ids[shard_index]
            live_count = group_live[shard_index]

            def per_slot(state_pair, slot_index):
                cell_acc, gene_inner = state_pair
                gene_start = slot_ids[slot_index] * BLOCK
                block_rows = lax.dynamic_slice_in_dim(group_weight, gene_start, BLOCK, 0)
                rate_tile = lax.dot_general(cell_rows, block_rows, (((1,), (1,)), ((), ())), preferred_element_type=jnp.float32)
                ratio_tile = count_tiles[slot_index].astype(jnp.float32) / rate_tile
                ratio_tile = jnp.where(slot_index < live_count, ratio_tile, jnp.float32(0.0)).astype(jnp.bfloat16)
                cell_acc = cell_acc + jnp.dot(ratio_tile, block_rows, preferred_element_type=jnp.float32)
                gene_term = lax.dot_general(ratio_tile, cell_rows, (((0,), (0,)), ((), ())), preferred_element_type=jnp.float32)
                previous = lax.dynamic_slice_in_dim(gene_inner, gene_start, BLOCK, 0)
                gene_inner = lax.dynamic_update_slice_in_dim(gene_inner, previous + gene_term, gene_start, 0)
                return (cell_acc, gene_inner), None

            start_pair = (jnp.zeros((C_DEV, K), jnp.float32), gene_acc)
            (cell_acc, gene_acc), unused = lax.scan(per_slot, start_pair, jnp.arange(SLOTS, dtype=jnp.int32))
            return gene_acc, cell_acc

        gene_acc, cell_parts = lax.scan(per_shard, jnp.zeros((GROUP_GENES, K), jnp.float32), jnp.arange(SHARDS, dtype=jnp.int32))
        cell_stat = cell_stat + cell_parts.reshape(CELLS, K)
        gene_parts.append(gene_acc.reshape(SHARDS, 1, OWN, K))
    gene_stat = jnp.concatenate(gene_parts, axis=1).reshape(G, K)
    log_theta_shape = jnp.log(0.3 + theta_weight.astype(jnp.float32) * cell_stat)
    log_theta_rate = jnp.log(cell_activity[:, None] + beta_total[None, :])
    log_beta_shape = jnp.log(0.3 + beta_weight.astype(jnp.float32) * gene_stat)
    log_beta_rate = jnp.log(gene_activity[:, None] + theta_total[None, :])
    return log_theta_shape, log_theta_rate, log_beta_shape, log_beta_rate
```

```python
import functools

import jax
import jax.numpy as jnp
from jax import lax
from jax.experimental import pallas as pl
from jax.experimental.pallas import tpu as pltpu
from jax.sharding import Mesh, PartitionSpec as P

F32 = jnp.float32
BF16 = jnp.bfloat16
VMEM = pl.BlockSpec(memory_space=pltpu.VMEM)
SMEM = pl.BlockSpec(memory_space=pltpu.SMEM)
EXTRA = 16
CHUNK = 256


def params(mib):
    return pltpu.CompilerParams(vmem_limit_bytes=mib * 1024 * 1024)


def digamma_series(value):
    shifted = value
    correction = jnp.zeros_like(value)
    for offset in range(6):
        correction = correction + 1.0 / shifted
        shifted = shifted + 1.0
    inverse = 1.0 / shifted
    square = inverse * inverse
    series = (
        jnp.log(shifted)
        - 0.5 * inverse
        - square * (1.0 / 12.0 - square * (1.0 / 120.0 - square * (1.0 / 252.0)))
    )
    return series - correction


def split_rows(total):
    high = total.astype(BF16).astype(F32)
    middle = (total - high).astype(BF16).astype(F32)
    low = total - high - middle
    row = lax.broadcasted_iota(jnp.int32, (EXTRA, total.shape[1]), 0)
    block = jnp.where(row == 0, high, jnp.where(row == 1, middle, jnp.where(row == 2, low, 0.0)))
    return block.astype(BF16)


def row_total(block):
    return jnp.sum(block.astype(F32), axis=0, keepdims=True)


def weights_kernel(ts_ref, tr_ref, bs_ref, br_ref, cell_ref, gene_ref):
    copies, rows = cell_ref.shape[0], ts_ref.shape[0]
    weight = jnp.exp(digamma_series(ts_ref[...]) - jnp.log(tr_ref[...])).astype(BF16)
    extra = split_rows(jnp.sum(ts_ref[...] / tr_ref[...], axis=0, keepdims=True))
    for copy in range(copies):
        cell_ref[copy, :rows] = weight
        cell_ref[copy, rows:] = extra
    genes = bs_ref.shape[0]
    gene_ref[:genes] = jnp.exp(digamma_series(bs_ref[...]) - jnp.log(br_ref[...])).astype(BF16)
    gene_ref[genes:] = split_rows(jnp.sum(bs_ref[...] / br_ref[...], axis=0, keepdims=True))


def main_kernel(
    ids_ref, live_ref, cell_ref, own_ref, oth_ref, counts_ref,
    cell_out, keep_out, send_out,
    rows_s, cols_s, acc_s, gene_s,
):
    step = pl.program_id(0)
    parts, padded, width = cell_ref.shape
    part = padded - EXTRA
    block = own_ref.shape[1] - EXTRA
    sides = own_ref.shape[0]
    cells = parts * part
    live = live_ref[0]
    my_y, my_x, my_core = lax.axis_index("y"), lax.axis_index("x"), lax.axis_index("core")

    @pl.when(step == 0)
    def _():
        for index in range(parts):
            rows = cell_ref[index, :part]
            rows_s[pl.ds(index * part, part), :] = rows
            cols_s[:, pl.ds(index * part, part)] = rows.T
        acc_s[...] = jnp.zeros_like(acc_s)
        gene_s[...] = jnp.zeros_like(gene_s)

    def place(slot):
        index = ids_ref[slot]
        core, x, y = index % 2, (index // 2) % 4, index // 8
        spot = ((my_y - y + 4) % 4) * 4 + (my_x - x + 4) % 4
        return index, core == my_core, spot

    def block_of(slot):
        _, mine, spot = place(slot)
        return jnp.where(mine, own_ref[spot, :block], oth_ref[spot, :block])

    @pl.when(2 * step < live)
    def _():
        second = 2 * step + 1 < live
        pair = jnp.concatenate([block_of(2 * step), block_of(2 * step + 1)], axis=0)
        total = jnp.zeros((width, 2 * block), F32)
        for start in range(0, cells, CHUNK):
            here = pl.ds(start, CHUNK)
            rate = lax.dot_general(
                rows_s[here, :], pair, (((1,), (1,)), ((), ())), preferred_element_type=F32
            )
            first_ratio = counts_ref[0, here, :].astype(F32) / rate[:, :block]
            second_ratio = counts_ref[1, here, :].astype(F32) / rate[:, block:]
            second_ratio = jnp.where(second, second_ratio, 0.0)
            ratio = jnp.concatenate([first_ratio, second_ratio], axis=1).astype(BF16)
            acc_s[here, :] += jnp.dot(ratio, pair, preferred_element_type=F32)
            total += jnp.dot(cols_s[:, here], ratio, preferred_element_type=F32)
        total = total.T

        def store(slot, value):
            index, mine, _ = place(slot)
            gene_s[jnp.where(mine, 0, 1), index // 2] = value

        store(2 * step, total[:block])

        @pl.when(second)
        def _():
            store(2 * step + 1, total[block:])

    @pl.when(step == pl.num_programs(0) - 1)
    def _():
        theta = row_total(cell_ref[:, part:].reshape(parts * EXTRA, width))
        beta = row_total(own_ref[:, block:].reshape(sides * EXTRA, width))
        beta += row_total(oth_ref[:, block:].reshape(sides * EXTRA, width))
        theta, beta = split_rows(theta), split_rows(beta)
        for index in range(parts):
            cell_out[index, :part] = acc_s[pl.ds(index * part, part), :].astype(BF16)
            cell_out[index, part:] = beta
        for index in range(sides):
            keep_out[index, :block] = gene_s[0, index]
            keep_out[index, block:] = theta.astype(F32)
            send_out[index, :block] = gene_s[1, index].astype(BF16)
            send_out[index, block:] = theta


def main_call(ids, live, cell_rows, own, other, counts):
    slots, cells, block = counts.shape
    parts, padded, width = cell_rows.shape
    sides, tall, _ = own.shape

    def counts_index(step, ids, live):
        return (jnp.minimum(step, (live[0] - 1) // 2), 0, 0)

    def whole(shape):
        return pl.BlockSpec(shape, lambda step, ids, live: (0,) * len(shape))

    return pl.pallas_call(
        main_kernel,
        grid_spec=pltpu.PrefetchScalarGridSpec(
            num_scalar_prefetch=2,
            grid=(slots // 2,),
            in_specs=[VMEM, VMEM, VMEM, pl.BlockSpec((2, cells, block), counts_index)],
            out_specs=[VMEM, VMEM, VMEM],
            scratch_shapes=[
                pltpu.VMEM((cells, width), BF16),
                pltpu.VMEM((width, cells), BF16),
                pltpu.VMEM((cells, width), F32),
                pltpu.VMEM((2, sides, block, width), F32),
            ],
        ),
        out_shape=[
            jax.ShapeDtypeStruct((parts, padded, width), BF16),
            jax.ShapeDtypeStruct((sides, tall, width), F32),
            jax.ShapeDtypeStruct((sides, tall, width), BF16),
        ],
        compiler_params=params(32),
    )(ids, live, cell_rows, own, other, counts)


def core_sum_kernel(keep_ref, got_ref, mine_ref, *send_refs):
    my_x = lax.axis_index("x")
    for y in range(4):
        for step in range(4):
            spot = y * 4 + (my_x + step) % 4
            value = keep_ref[spot] + got_ref[spot].astype(F32)
            if step == 0:
                mine_ref[y] = value
            else:
                send_refs[step - 1][y] = respread(value).astype(BF16)


def respread(value):
    rows = value.shape[0] - EXTRA
    return jnp.concatenate([value[:rows].astype(BF16), split_rows(row_total(value[rows:]))], axis=0)


def x_sum_kernel(keep_ref, a_ref, b_ref, c_ref, mine_ref, *send_refs):
    my_y = lax.axis_index("y")
    for step in range(4):
        spot = (my_y + step) % 4
        value = keep_ref[spot] + a_ref[spot].astype(F32)
        value += b_ref[spot].astype(F32) + c_ref[spot].astype(F32)
        if step == 0:
            mine_ref[...] = value
        else:
            send_refs[step - 1][...] = respread(value)


def finish(weight, stat, activity, total, shape_ref, rate_ref):
    rows, width = stat.shape
    shape_ref[...] = jnp.log(0.3 + weight.astype(F32) * stat)
    for start in range(0, rows, 128):
        here = pl.ds(start, 128)
        column = jnp.broadcast_to(activity[:, start : start + 128], (width, 128)).T
        rate_ref[here, :] = jnp.log(column + total)


def gene_finish_kernel(keep_ref, a_ref, b_ref, c_ref, weight_ref, act_ref, shape_ref, rate_ref):
    value = keep_ref[...] + a_ref[...].astype(F32)
    value += b_ref[...].astype(F32) + c_ref[...].astype(F32)
    rows = value.shape[0] - EXTRA
    total = row_total(value[rows:])
    finish(weight_ref[:rows], value[:rows], act_ref[...], total, shape_ref, rate_ref)


def cell_finish_kernel(got_ref, weight_ref, act_ref, shape_ref, rate_ref):
    parts = got_ref.shape[0]
    rows = got_ref.shape[1] - EXTRA
    value = got_ref[0].astype(F32)
    for index in range(1, parts):
        value += got_ref[index].astype(F32)
    total = row_total(value[rows:])
    finish(weight_ref[0, :rows], value[:rows], act_ref[...], total, shape_ref, rate_ref)


def simple_call(kernel, out_shape, *args, mib=16):
    return pl.pallas_call(
        kernel,
        in_specs=[VMEM] * len(args),
        out_specs=[VMEM] * len(out_shape),
        out_shape=out_shape,
        compiler_params=params(mib),
    )(*args)


def shift(axis, size, step):
    pairs = [(index, (index + step) % size) for index in range(size)]
    return functools.partial(lax.ppermute, axis_name=axis, perm=pairs)


def on_device(
    theta_shape,
    theta_rate,
    cell_activity,
    beta_shape,
    beta_rate,
    gene_activity,
    block_ids,
    live_blocks,
    counts,
):
    cells, width = theta_shape.shape
    genes = beta_shape.shape[0]
    tall = genes + EXTRA
    struct = jax.ShapeDtypeStruct
    cell_pay, gene_pay = simple_call(
        weights_kernel,
        [struct((8, cells + EXTRA, width), BF16), struct((tall, width), BF16)],
        theta_shape, theta_rate, beta_shape, beta_rate,
    )
    cell_rows = lax.all_to_all(cell_pay, "z", 0, 0)
    along_x = jnp.stack([gene_pay] + [shift("x", 4, step)(gene_pay) for step in (1, 2, 3)])
    own = jnp.concatenate([along_x] + [shift("y", 4, step)(along_x) for step in (1, 2, 3)])
    other = shift("core", 2, 1)(own)

    cell_part, keep, send = main_call(
        block_ids[0, 0], live_blocks[0], cell_rows, own, other, counts[0]
    )
    cell_got = lax.all_to_all(cell_part, "z", 0, 0)
    got = shift("core", 2, 1)(send)
    keep, *sends = simple_call(
        core_sum_kernel,
        [struct((4, tall, width), F32)] + [struct((4, tall, width), BF16)] * 3,
        keep, got,
    )
    gots = [shift("x", 4, step)(sends[step - 1]) for step in (1, 2, 3)]
    keep, *sends = simple_call(
        x_sum_kernel,
        [struct((tall, width), F32)] + [struct((tall, width), BF16)] * 3,
        keep, *gots,
    )
    gots = [shift("y", 4, step)(sends[step - 1]) for step in (1, 2, 3)]
    log_beta_shape, log_beta_rate = simple_call(
        gene_finish_kernel, [struct((genes, width), F32)] * 2,
        keep, *gots, gene_pay, gene_activity.reshape(1, genes),
    )
    log_theta_shape, log_theta_rate = simple_call(
        cell_finish_kernel, [struct((cells, width), F32)] * 2,
        cell_got, cell_pay, cell_activity.reshape(1, cells),
    )
    return (log_theta_shape, log_theta_rate, log_beta_shape, log_beta_rate)


def solution(mesh):
    fine = Mesh(mesh.devices.reshape(4, 4, 2, 8), ("y", "x", "core", "z"))
    cells = ("y", "x", "core")
    every = cells + ("z",)
    in_specs = (
        P(every, None),
        P(every, None),
        P(every),
        P(every, None),
        P(every, None),
        P(every),
        P("z", cells, None),
        P("z", cells),
        P("z", None, cells, None),
    )
    out_specs = (P(every, None),) * 4
    return jax.shard_map(
        on_device, mesh=fine, in_specs=in_specs, out_specs=out_specs, check_vma=False
    )
```

```python
import jax
import jax.numpy as jnp
from jax import lax
from jax.experimental import pallas as pl
from jax.experimental.pallas import tpu as pltpu
from jax.sharding import Mesh, PartitionSpec as P

F32 = jnp.float32
BF16 = jnp.bfloat16
VMEM = pl.BlockSpec(memory_space=pltpu.VMEM)
HBM = pl.BlockSpec(memory_space=pltpu.HBM)
EXTRA = 16
CHUNK = 1024
GROUP = 4


def params(mib):
    return pltpu.CompilerParams(vmem_limit_bytes=mib * 1024 * 1024)


def digamma_series(value):
    shifted = value
    correction = jnp.zeros_like(value)
    for offset in range(6):
        correction = correction + 1.0 / shifted
        shifted = shifted + 1.0
    inverse = 1.0 / shifted
    square = inverse * inverse
    series = (
        jnp.log(shifted)
        - 0.5 * inverse
        - square * (1.0 / 12.0 - square * (1.0 / 120.0 - square * (1.0 / 252.0)))
    )
    return series - correction


def split_rows(total):
    high = total.astype(BF16).astype(F32)
    middle = (total - high).astype(BF16).astype(F32)
    low = total - high - middle
    row = lax.broadcasted_iota(jnp.int32, (EXTRA, total.shape[1]), 0)
    block = jnp.where(row == 0, high, jnp.where(row == 1, middle, jnp.where(row == 2, low, 0.0)))
    return block.astype(BF16)


def row_total(block):
    return jnp.sum(block.astype(F32), axis=0, keepdims=True)


def weights_kernel(ts_hbm, tr_hbm, bs_hbm, br_hbm, cell_ref, gene_ref, ts_s, tr_s, bs_s, br_s, sems):
    pairs = ((bs_hbm, bs_s), (br_hbm, br_s), (ts_hbm, ts_s), (tr_hbm, tr_s))
    moves = [pltpu.make_async_copy(*pair, sems.at[index]) for index, pair in enumerate(pairs)]
    for move in moves:
        move.start()
    moves[0].wait()
    moves[1].wait()
    shape, rate = bs_s[...], br_s[...]
    genes = shape.shape[0]
    gene_ref[:genes] = jnp.exp(digamma_series(shape) - jnp.log(rate)).astype(BF16)
    gene_ref[genes:] = split_rows(jnp.sum(shape / rate, axis=0, keepdims=True))
    moves[2].wait()
    moves[3].wait()
    shape, rate = ts_s[...], tr_s[...]
    copies, cells = cell_ref.shape[0], shape.shape[0]
    weight = jnp.exp(digamma_series(shape) - jnp.log(rate)).astype(BF16)
    extra = split_rows(jnp.sum(shape / rate, axis=0, keepdims=True))
    for copy in range(copies):
        cell_ref[copy, :cells] = weight
        cell_ref[copy, cells:] = extra


def weights_call(theta_shape, theta_rate, beta_shape, beta_rate):
    cells, width = theta_shape.shape
    genes = beta_shape.shape[0]
    return pl.pallas_call(
        weights_kernel,
        in_specs=[HBM] * 4,
        out_specs=[VMEM] * 2,
        out_shape=[
            jax.ShapeDtypeStruct((8, cells + EXTRA, width), BF16),
            jax.ShapeDtypeStruct((genes + EXTRA, width), BF16),
        ],
        scratch_shapes=[pltpu.VMEM((cells, width), F32)] * 2
        + [pltpu.VMEM((genes, width), F32)] * 2
        + [pltpu.SemaphoreType.DMA((4,))],
        compiler_params=params(16),
    )(theta_shape, theta_rate, beta_shape, beta_rate)


def main_kernel(
    ids_ref, live_ref, cell_ref, own_ref, oth_ref, counts_ref,
    cell_out, keep_out, send_out,
    ids_s, live_s, counts_s, rows_s, cols_s, acc_s, gene_s, sems, id_sem, live_sem,
):
    parts, padded, width = cell_ref.shape
    part = padded - EXTRA
    block = own_ref.shape[1] - EXTRA
    sides = own_ref.shape[0]
    cells = parts * part
    groups = counts_ref.shape[0] // GROUP
    my_y, my_x, my_core = lax.axis_index("y"), lax.axis_index("x"), lax.axis_index("core")

    def fetch(group):
        here = pl.ds(group * GROUP, GROUP)
        return pltpu.make_async_copy(counts_ref.at[here], counts_s.at[here], sems.at[group])

    live_copy = pltpu.make_async_copy(live_ref, live_s, live_sem)
    ids_copy = pltpu.make_async_copy(ids_ref, ids_s, id_sem)
    live_copy.start()
    ids_copy.start()
    fetch(0).start()
    for index in range(parts):
        rows = cell_ref[index, :part]
        rows_s[pl.ds(index * part, part), :] = rows
        cols_s[:, pl.ds(index * part, part)] = rows.T
    gene_s[...] = jnp.zeros_like(gene_s)
    live_copy.wait()
    ids_copy.wait()
    live = live_s[0, 0]
    for group in range(1, groups):
        @pl.when(GROUP * group < live)
        def _():
            fetch(group).start()

    def place(slot):
        index = ids_s[0, 0, slot]
        core, x, y = index % 2, (index // 2) % 4, index // 8
        from_x, from_y = (my_x - x + 4) % 4, (my_y - y + 4) % 4
        spot = jnp.where(core == 0, from_y * 4 + from_x, from_x * 4 + from_y)
        return index, core == my_core, spot

    def block_of(slot):
        _, mine, spot = place(slot)
        return jnp.where(mine, own_ref[spot, :block], oth_ref[spot, :block])

    for group in range(groups):
        @pl.when(GROUP * group < live)
        def _():
            slots = [GROUP * group + index for index in range(GROUP)]
            alive = [slot < live for slot in slots]
            pair = jnp.concatenate([block_of(slot) for slot in slots], axis=0)
            fetch(group).wait()
            total = jnp.zeros((width, GROUP * block), F32)
            for start in range(0, cells, CHUNK):
                here = pl.ds(start, CHUNK)
                rate = lax.dot_general(
                    rows_s[here, :], pair, (((1,), (1,)), ((), ())), preferred_element_type=F32
                )
                ratios = []
                for index in range(GROUP):
                    columns = slice(index * block, (index + 1) * block)
                    ratio = counts_s[slots[index], here, :].astype(F32) / rate[:, columns]
                    if slots[index] > 1:
                        ratio = jnp.where(alive[index], ratio, 0.0)
                    ratios.append(ratio.astype(BF16))
                ratio = jnp.concatenate(ratios, axis=1)
                term = jnp.dot(ratio, pair, preferred_element_type=F32)
                if group == 0:
                    acc_s[here, :] = term
                else:
                    acc_s[here, :] += term
                total += jnp.dot(cols_s[:, here], ratio, preferred_element_type=F32)
            total = total.T
            for k in range(GROUP):
                @pl.when(alive[k])
                def _():
                    index, mine, _ = place(slots[k])
                    gene_s[jnp.where(mine, 0, 1), index // 2] = total[k * block : (k + 1) * block]

    theta = row_total(cell_ref[:, part:].reshape(parts * EXTRA, width))
    beta = row_total(own_ref[:, block:].reshape(sides * EXTRA, width))
    beta += row_total(oth_ref[:, block:].reshape(sides * EXTRA, width))
    theta, beta = split_rows(theta), split_rows(beta)
    for index in range(parts):
        cell_out[index, :part] = acc_s[pl.ds(index * part, part), :].astype(BF16)
        cell_out[index, part:] = beta
    for index in range(sides):
        keep_out[index, :block] = gene_s[0, index]
        keep_out[index, block:] = theta.astype(F32)
        send_out[index, :block] = gene_s[1, index].astype(BF16)
        send_out[index, block:] = theta


def main_call(ids, live, cell_rows, own, other, counts):
    slots, cells, block = counts.shape
    parts, padded, width = cell_rows.shape
    sides, tall, _ = own.shape
    return pl.pallas_call(
        main_kernel,
        in_specs=[HBM, HBM, VMEM, VMEM, VMEM, HBM],
        out_specs=[VMEM, VMEM, VMEM],
        scratch_shapes=[
            pltpu.SMEM(ids.shape, jnp.int32),
            pltpu.SMEM(live.shape, jnp.int32),
            pltpu.VMEM((slots, cells, block), BF16),
            pltpu.VMEM((cells, width), BF16),
            pltpu.VMEM((width, cells), BF16),
            pltpu.VMEM((cells, width), F32),
            pltpu.VMEM((2, sides, block, width), F32),
            pltpu.SemaphoreType.DMA((slots // GROUP,)),
            pltpu.SemaphoreType.DMA,
            pltpu.SemaphoreType.DMA,
        ],
        out_shape=[
            jax.ShapeDtypeStruct((parts, padded, width), BF16),
            jax.ShapeDtypeStruct((sides, tall, width), F32),
            jax.ShapeDtypeStruct((sides, tall, width), BF16),
        ],
        compiler_params=params(48),
    )(ids, live, cell_rows, own, other, counts)


def first_and_second():
    my_y, my_x, core = lax.axis_index("y"), lax.axis_index("x"), lax.axis_index("core")
    return core, jnp.where(core == 0, my_x, my_y), jnp.where(core == 0, my_y, my_x)


def core_sum_kernel(keep_ref, got_ref, mine_ref, *send_refs):
    core, first, _ = first_and_second()
    for row in range(4):
        for step in range(4):
            along = (first + step) % 4
            spot = jnp.where(core == 0, row * 4 + along, along * 4 + row)
            value = keep_ref[spot] + got_ref[spot].astype(F32)
            if step == 0:
                mine_ref[row] = value
            else:
                send_refs[step - 1][row] = respread(value)


def respread(value):
    rows = value.shape[0] - EXTRA
    return jnp.concatenate([value[:rows].astype(BF16), split_rows(row_total(value[rows:]))], axis=0)


def first_sum_kernel(keep_ref, a_ref, b_ref, c_ref, mine_ref, *send_refs):
    _, _, second = first_and_second()
    for step in range(4):
        spot = (second + step) % 4
        value = keep_ref[spot] + a_ref[spot].astype(F32)
        value += b_ref[spot].astype(F32) + c_ref[spot].astype(F32)
        if step == 0:
            mine_ref[...] = value
        else:
            send_refs[step - 1][...] = respread(value)


def finish(weight, stat, activity, total, shape_ref, rate_ref):
    rows, width = stat.shape
    shape_ref[...] = jnp.log(0.3 + weight.astype(F32) * stat)
    for start in range(0, rows, 128):
        here = pl.ds(start, 128)
        column = jnp.broadcast_to(activity[:, start : start + 128], (width, 128)).T
        rate_ref[here, :] = jnp.log(column + total)


def gene_finish_kernel(keep_ref, a_ref, b_ref, c_ref, weight_ref, act_ref, shape_ref, rate_ref):
    value = keep_ref[...] + a_ref[...].astype(F32)
    value += b_ref[...].astype(F32) + c_ref[...].astype(F32)
    rows = value.shape[0] - EXTRA
    total = row_total(value[rows:])
    finish(weight_ref[:rows], value[:rows], act_ref[...], total, shape_ref, rate_ref)


def cell_finish_kernel(got_ref, weight_ref, act_ref, shape_ref, rate_ref):
    parts = got_ref.shape[0]
    rows = got_ref.shape[1] - EXTRA
    value = got_ref[0].astype(F32)
    for index in range(1, parts):
        value += got_ref[index].astype(F32)
    total = row_total(value[rows:])
    finish(weight_ref[0, :rows], value[:rows], act_ref[...], total, shape_ref, rate_ref)


def simple_call(kernel, out_shape, *args, mib=16):
    return pl.pallas_call(
        kernel,
        in_specs=[VMEM] * len(args),
        out_specs=[VMEM] * len(out_shape),
        out_shape=out_shape,
        compiler_params=params(mib),
    )(*args)


def shift(stage, step, value):
    pairs = []
    for y in range(4):
        for x in range(4):
            for core in range(2):
                if core == stage:
                    to_y, to_x = y, (x + step) % 4
                else:
                    to_y, to_x = (y + step) % 4, x
                pairs.append(((y * 4 + x) * 2 + core, (to_y * 4 + to_x) * 2 + core))
    return lax.ppermute(value, ("y", "x", "core"), pairs)


def swap_cores(value):
    return lax.ppermute(value, "core", [(0, 1), (1, 0)])


def on_device(
    theta_shape,
    theta_rate,
    cell_activity,
    beta_shape,
    beta_rate,
    gene_activity,
    block_ids,
    live_blocks,
    counts,
):
    cells, width = theta_shape.shape
    genes = beta_shape.shape[0]
    tall = genes + EXTRA
    struct = jax.ShapeDtypeStruct
    steps = (1, 2, 3)
    cell_pay, gene_pay = weights_call(theta_shape, theta_rate, beta_shape, beta_rate)
    cell_rows = lax.all_to_all(cell_pay, "z", 0, 0)
    line = jnp.stack([gene_pay] + [shift(0, step, gene_pay) for step in steps])
    own = jnp.concatenate([line] + [shift(1, step, line) for step in steps])
    other = swap_cores(own)

    cell_part, keep, send = main_call(block_ids, live_blocks, cell_rows, own, other, counts[0])
    cell_got = lax.all_to_all(cell_part, "z", 0, 0)
    keep, *sends = simple_call(
        core_sum_kernel,
        [struct((4, tall, width), F32)] + [struct((4, tall, width), BF16)] * 3,
        keep, swap_cores(send),
    )
    gots = [shift(0, step, sends[step - 1]) for step in steps]
    keep, *sends = simple_call(
        first_sum_kernel,
        [struct((tall, width), F32)] + [struct((tall, width), BF16)] * 3,
        keep, *gots,
    )
    gots = [shift(1, step, sends[step - 1]) for step in steps]
    log_theta = simple_call(
        cell_finish_kernel, [struct((cells, width), F32)] * 2,
        cell_got, cell_pay, cell_activity.reshape(1, cells),
    )
    gots, log_theta = lax.optimization_barrier((gots, log_theta))
    log_beta = simple_call(
        gene_finish_kernel, [struct((genes, width), F32)] * 2,
        keep, *gots, gene_pay, gene_activity.reshape(1, genes),
    )
    return (*log_theta, *log_beta)


def solution(mesh):
    fine = Mesh(mesh.devices.reshape(4, 4, 2, 8), ("y", "x", "core", "z"))
    cells = ("y", "x", "core")
    every = cells + ("z",)
    in_specs = (
        P(every, None),
        P(every, None),
        P(every),
        P(every, None),
        P(every, None),
        P(every),
        P("z", cells, None),
        P("z", cells),
        P("z", None, cells, None),
    )
    out_specs = (P(every, None),) * 4
    return jax.shard_map(
        on_device, mesh=fine, in_specs=in_specs, out_specs=out_specs, check_vma=False
    )
```

```python
import jax
import jax.numpy as jnp
from jax import lax
from jax.experimental import pallas as pl
from jax.experimental.pallas import tpu as pltpu
from jax.sharding import Mesh, PartitionSpec as P

F32 = jnp.float32
BF16 = jnp.bfloat16
VMEM = pl.BlockSpec(memory_space=pltpu.VMEM)
HBM = pl.BlockSpec(memory_space=pltpu.HBM)
EXTRA = 16
CHUNK = 1024
GROUP = 4


def params(mib):
    return pltpu.CompilerParams(vmem_limit_bytes=mib * 1024 * 1024)


def digamma_series(value):
    shifted = value
    correction = jnp.zeros_like(value)
    for offset in range(6):
        correction = correction + 1.0 / shifted
        shifted = shifted + 1.0
    inverse = 1.0 / shifted
    square = inverse * inverse
    series = (
        jnp.log(shifted)
        - 0.5 * inverse
        - square * (1.0 / 12.0 - square * (1.0 / 120.0 - square * (1.0 / 252.0)))
    )
    return series - correction


def split_rows(total):
    high = total.astype(BF16).astype(F32)
    middle = (total - high).astype(BF16).astype(F32)
    low = total - high - middle
    row = lax.broadcasted_iota(jnp.int32, (EXTRA, total.shape[1]), 0)
    block = jnp.where(row == 0, high, jnp.where(row == 1, middle, jnp.where(row == 2, low, 0.0)))
    return block.astype(BF16)


def row_total(block):
    return jnp.sum(block.astype(F32), axis=0, keepdims=True)


def weights_kernel(ts_hbm, tr_hbm, bs_hbm, br_hbm, cell_ref, gene_ref, ts_s, tr_s, bs_s, br_s, sems):
    pairs = ((bs_hbm, bs_s), (br_hbm, br_s), (ts_hbm, ts_s), (tr_hbm, tr_s))
    moves = [pltpu.make_async_copy(*pair, sems.at[index]) for index, pair in enumerate(pairs)]
    for move in moves:
        move.start()
    moves[0].wait()
    moves[1].wait()
    shape, rate = bs_s[...], br_s[...]
    genes = shape.shape[0]
    gene_ref[:genes] = jnp.exp(digamma_series(shape) - jnp.log(rate)).astype(BF16)
    gene_ref[genes:] = split_rows(jnp.sum(shape / rate, axis=0, keepdims=True))
    moves[2].wait()
    moves[3].wait()
    shape, rate = ts_s[...], tr_s[...]
    copies, cells = cell_ref.shape[0], shape.shape[0]
    weight = jnp.exp(digamma_series(shape) - jnp.log(rate)).astype(BF16)
    extra = split_rows(jnp.sum(shape / rate, axis=0, keepdims=True))
    for copy in range(copies):
        cell_ref[copy, :cells] = weight
        cell_ref[copy, cells:] = extra


def weights_call(theta_shape, theta_rate, beta_shape, beta_rate):
    cells, width = theta_shape.shape
    genes = beta_shape.shape[0]
    return pl.pallas_call(
        weights_kernel,
        in_specs=[HBM] * 4,
        out_specs=[VMEM] * 2,
        out_shape=[
            jax.ShapeDtypeStruct((8, cells + EXTRA, width), BF16),
            jax.ShapeDtypeStruct((genes + EXTRA, width), BF16),
        ],
        scratch_shapes=[pltpu.VMEM((cells, width), F32)] * 2
        + [pltpu.VMEM((genes, width), F32)] * 2
        + [pltpu.SemaphoreType.DMA((4,))],
        compiler_params=pltpu.CompilerParams(vmem_limit_bytes=55152 * 1024),
    )(theta_shape, theta_rate, beta_shape, beta_rate)


def main_kernel(
    ids_ref, live_ref, cell_ref, own_ref, oth_ref, counts_ref,
    cell_out, keep_out, send_out,
    ids_s, live_s, counts_s, rows_s, cols_s, acc_s, gene_s, sems, id_sem, live_sem,
):
    parts, padded, width = cell_ref.shape
    part = padded - EXTRA
    block = own_ref.shape[1] - EXTRA
    sides = own_ref.shape[0]
    cells = parts * part
    groups = counts_ref.shape[0] // GROUP
    my_y, my_x, my_core = lax.axis_index("y"), lax.axis_index("x"), lax.axis_index("core")

    def fetch(group):
        here = pl.ds(group * GROUP, GROUP)
        return pltpu.make_async_copy(counts_ref.at[here], counts_s.at[here], sems.at[group])

    live_copy = pltpu.make_async_copy(live_ref, live_s, live_sem)
    ids_copy = pltpu.make_async_copy(ids_ref, ids_s, id_sem)
    live_copy.start()
    ids_copy.start()
    fetch(0).start()
    for index in range(parts):
        rows = cell_ref[index, :part]
        rows_s[pl.ds(index * part, part), :] = rows
        cols_s[:, pl.ds(index * part, part)] = rows.T
    gene_s[...] = jnp.zeros_like(gene_s)
    live_copy.wait()
    ids_copy.wait()
    live = live_s[0, 0]
    for group in range(1, groups):
        @pl.when(GROUP * group < live)
        def _():
            fetch(group).start()

    def place(slot):
        index = ids_s[0, 0, slot]
        core, x, y = index % 2, (index // 2) % 4, index // 8
        from_x, from_y = (my_x - x + 4) % 4, (my_y - y + 4) % 4
        spot = jnp.where(core == 0, from_y * 4 + from_x, from_x * 4 + from_y)
        return index, core == my_core, spot

    def block_of(slot):
        _, mine, spot = place(slot)
        return jnp.where(mine, own_ref[spot, :block], oth_ref[spot, :block])

    for group in range(groups):
        @pl.when(GROUP * group < live)
        def _():
            slots = [GROUP * group + index for index in range(GROUP)]
            alive = [slot < live for slot in slots]
            pair = jnp.concatenate([block_of(slot) for slot in slots], axis=0)
            fetch(group).wait()
            total = jnp.zeros((width, GROUP * block), F32)
            for start in range(0, cells, CHUNK):
                here = pl.ds(start, CHUNK)
                rate = lax.dot_general(
                    rows_s[here, :], pair, (((1,), (1,)), ((), ())), preferred_element_type=F32
                )
                ratios = []
                for index in range(GROUP):
                    columns = slice(index * block, (index + 1) * block)
                    ratio = counts_s[slots[index], here, :].astype(F32) / rate[:, columns]
                    if slots[index] > 1:
                        ratio = jnp.where(alive[index], ratio, 0.0)
                    ratios.append(ratio.astype(BF16))
                ratio = jnp.concatenate(ratios, axis=1)
                term = jnp.dot(ratio, pair, preferred_element_type=F32)
                if group == 0:
                    acc_s[here, :] = term
                else:
                    acc_s[here, :] += term
                total += jnp.dot(cols_s[:, here], ratio, preferred_element_type=F32)
            total = total.T
            for k in range(GROUP):
                @pl.when(alive[k])
                def _():
                    index, mine, _ = place(slots[k])
                    gene_s[jnp.where(mine, 0, 1), index // 2] = total[k * block : (k + 1) * block]

    theta = row_total(cell_ref[:, part:].reshape(parts * EXTRA, width))
    beta = row_total(own_ref[:, block:].reshape(sides * EXTRA, width))
    beta += row_total(oth_ref[:, block:].reshape(sides * EXTRA, width))
    theta, beta = split_rows(theta), split_rows(beta)
    for index in range(parts):
        cell_out[index, :part] = acc_s[pl.ds(index * part, part), :].astype(BF16)
        cell_out[index, part:] = beta
    for index in range(sides):
        keep_out[index, :block] = gene_s[0, index]
        keep_out[index, block:] = theta.astype(F32)
        send_out[index, :block] = gene_s[1, index].astype(BF16)
        send_out[index, block:] = theta


def main_call(ids, live, cell_rows, own, other, counts):
    slots, cells, block = counts.shape
    parts, padded, width = cell_rows.shape
    sides, tall, _ = own.shape
    return pl.pallas_call(
        main_kernel,
        in_specs=[HBM, HBM, VMEM, VMEM, VMEM, HBM],
        out_specs=[VMEM, VMEM, VMEM],
        scratch_shapes=[
            pltpu.SMEM(ids.shape, jnp.int32),
            pltpu.SMEM(live.shape, jnp.int32),
            pltpu.VMEM((slots, cells, block), BF16),
            pltpu.VMEM((cells, width), BF16),
            pltpu.VMEM((width, cells), BF16),
            pltpu.VMEM((cells, width), F32),
            pltpu.VMEM((2, sides, block, width), F32),
            pltpu.SemaphoreType.DMA((slots // GROUP,)),
            pltpu.SemaphoreType.DMA,
            pltpu.SemaphoreType.DMA,
        ],
        out_shape=[
            jax.ShapeDtypeStruct((parts, padded, width), BF16),
            jax.ShapeDtypeStruct((sides, tall, width), F32),
            jax.ShapeDtypeStruct((sides, tall, width), BF16),
        ],
        compiler_params=params(48),
    )(ids, live, cell_rows, own, other, counts)


def first_and_second():
    my_y, my_x, core = lax.axis_index("y"), lax.axis_index("x"), lax.axis_index("core")
    return core, jnp.where(core == 0, my_x, my_y), jnp.where(core == 0, my_y, my_x)


def core_sum_kernel(keep_ref, got_ref, mine_ref, *send_refs):
    core, first, _ = first_and_second()
    for row in range(4):
        for step in range(4):
            along = (first + step) % 4
            spot = jnp.where(core == 0, row * 4 + along, along * 4 + row)
            value = keep_ref[spot] + got_ref[spot].astype(F32)
            if step == 0:
                mine_ref[row] = value
            else:
                send_refs[step - 1][row] = respread(value)


def respread(value):
    rows = value.shape[0] - EXTRA
    return jnp.concatenate([value[:rows].astype(BF16), split_rows(row_total(value[rows:]))], axis=0)


def first_sum_kernel(keep_ref, a_ref, b_ref, c_ref, mine_ref, *send_refs):
    _, _, second = first_and_second()
    for step in range(4):
        spot = (second + step) % 4
        value = keep_ref[spot] + a_ref[spot].astype(F32)
        value += b_ref[spot].astype(F32) + c_ref[spot].astype(F32)
        if step == 0:
            mine_ref[...] = value
        else:
            send_refs[step - 1][...] = respread(value)


def finish(weight, stat, activity, total, shape_ref, rate_ref):
    rows, width = stat.shape
    shape_ref[...] = jnp.log(0.3 + weight.astype(F32) * stat)
    for start in range(0, rows, 128):
        here = pl.ds(start, 128)
        column = jnp.broadcast_to(activity[:, start : start + 128], (width, 128)).T
        rate_ref[here, :] = jnp.log(column + total)


def gene_finish_kernel(keep_ref, a_ref, b_ref, c_ref, weight_ref, act_ref, shape_ref, rate_ref):
    value = keep_ref[...] + a_ref[...].astype(F32)
    value += b_ref[...].astype(F32) + c_ref[...].astype(F32)
    rows = value.shape[0] - EXTRA
    total = row_total(value[rows:])
    finish(weight_ref[:rows], value[:rows], act_ref[...], total, shape_ref, rate_ref)


def cell_finish_kernel(got_ref, weights_ref, act_ref, shape_ref, rate_ref):
    parts = got_ref.shape[0]
    rows = got_ref.shape[1] - EXTRA
    value = got_ref[0].astype(F32)
    for index in range(1, parts):
        value += got_ref[index].astype(F32)
    total = row_total(value[rows:])
    weight = weights_ref[lax.axis_index("z"), :rows]
    finish(weight, value[:rows], act_ref[...], total, shape_ref, rate_ref)


def simple_call(kernel, out_shape, *args, mib=16):
    return pl.pallas_call(
        kernel,
        in_specs=[VMEM] * len(args),
        out_specs=[VMEM] * len(out_shape),
        out_shape=out_shape,
        compiler_params=params(mib),
    )(*args)


def shift(stage, step, value):
    pairs = []
    for y in range(4):
        for x in range(4):
            for core in range(2):
                if core == stage:
                    to_y, to_x = y, (x + step) % 4
                else:
                    to_y, to_x = (y + step) % 4, x
                pairs.append(((y * 4 + x) * 2 + core, (to_y * 4 + to_x) * 2 + core))
    return lax.ppermute(value, ("y", "x", "core"), pairs)


def swap_cores(value):
    return lax.ppermute(value, "core", [(0, 1), (1, 0)])


def on_device(
    theta_shape,
    theta_rate,
    cell_activity,
    beta_shape,
    beta_rate,
    gene_activity,
    block_ids,
    live_blocks,
    counts,
):
    cells, width = theta_shape.shape
    genes = beta_shape.shape[0]
    tall = genes + EXTRA
    struct = jax.ShapeDtypeStruct
    steps = (1, 2, 3)
    cell_pay, gene_pay = weights_call(theta_shape, theta_rate, beta_shape, beta_rate)
    cell_rows = lax.all_to_all(cell_pay, "z", 0, 0)
    got = {step: shift(0, step, gene_pay) for step in steps}
    line = jnp.stack([gene_pay, got[1], got[2], got[3]])
    got = {step: shift(1, step, line) for step in steps}
    ids = jnp.maximum(block_ids, 0)
    got, ids = lax.optimization_barrier((got, ids))
    own = jnp.concatenate([line, got[1], got[2], got[3]])
    other = swap_cores(own)

    cell_part, keep, send = main_call(ids, live_blocks, cell_rows, own, other, counts[0])
    cell_got = lax.all_to_all(cell_part, "z", 0, 0)
    keep, *sends = simple_call(
        core_sum_kernel,
        [struct((4, tall, width), F32)] + [struct((4, tall, width), BF16)] * 3,
        keep, swap_cores(send),
    )
    gots = [shift(0, step, sends[step - 1]) for step in steps]
    keep, *sends = simple_call(
        first_sum_kernel,
        [struct((tall, width), F32)] + [struct((tall, width), BF16)] * 3,
        keep, *gots,
    )
    gots = [shift(1, step, sends[step - 1]) for step in steps]
    log_theta = simple_call(
        cell_finish_kernel, [struct((cells, width), F32)] * 2,
        cell_got, cell_rows, cell_activity.reshape(1, cells),
    )
    gots, log_theta = lax.optimization_barrier((gots, log_theta))
    log_beta = simple_call(
        gene_finish_kernel, [struct((genes, width), F32)] * 2,
        keep, *gots, gene_pay, gene_activity.reshape(1, genes),
    )
    return (*log_theta, *log_beta)


def solution(mesh):
    fine = Mesh(mesh.devices.reshape(4, 4, 2, 8), ("y", "x", "core", "z"))
    cells = ("y", "x", "core")
    every = cells + ("z",)
    in_specs = (
        P(every, None),
        P(every, None),
        P(every),
        P(every, None),
        P(every, None),
        P(every),
        P("z", cells, None),
        P("z", cells),
        P("z", None, cells, None),
    )
    out_specs = (P(every, None),) * 4
    return jax.shard_map(
        on_device, mesh=fine, in_specs=in_specs, out_specs=out_specs, check_vma=False
    )
```

```python
import jax
import jax.numpy as jnp
from jax import lax
from jax.experimental import pallas as pl
from jax.experimental.pallas import tpu as pltpu
from jax.sharding import Mesh, PartitionSpec as P

F32 = jnp.float32
BF16 = jnp.bfloat16
VMEM = pl.BlockSpec(memory_space=pltpu.VMEM)
HBM = pl.BlockSpec(memory_space=pltpu.HBM)
EXTRA = 16
CHUNK = 1024
GROUP = 4


def params(mib):
    return pltpu.CompilerParams(vmem_limit_bytes=mib * 1024 * 1024)


def digamma_series(value):
    shifted = value
    correction = jnp.zeros_like(value)
    for offset in range(6):
        correction = correction + 1.0 / shifted
        shifted = shifted + 1.0
    inverse = 1.0 / shifted
    square = inverse * inverse
    series = (
        jnp.log(shifted)
        - 0.5 * inverse
        - square * (1.0 / 12.0 - square * (1.0 / 120.0 - square * (1.0 / 252.0)))
    )
    return series - correction


def split_rows(beta, theta):
    row = lax.broadcasted_iota(jnp.int32, (EXTRA, beta.shape[1]), 0)
    block = jnp.zeros(row.shape, F32)
    for start, total in ((0, beta), (3, theta)):
        high = total.astype(BF16).astype(F32)
        middle = (total - high).astype(BF16).astype(F32)
        for index, part in enumerate((high, middle, total - high - middle)):
            block = jnp.where(row == start + index, part, block)
    return block.astype(BF16)


def row_totals(blocks):
    block = jnp.sum(blocks.astype(F32), axis=0)
    return jnp.sum(block[:3], axis=0, keepdims=True), jnp.sum(block[3:6], axis=0, keepdims=True)


def weights_kernel(ts_hbm, tr_hbm, bs_hbm, br_hbm, cell_ref, gene_ref, ts_s, tr_s, bs_s, br_s, sems):
    pairs = ((bs_hbm, bs_s), (br_hbm, br_s), (ts_hbm, ts_s), (tr_hbm, tr_s))
    moves = [pltpu.make_async_copy(*pair, sems.at[index]) for index, pair in enumerate(pairs)]
    for move in moves:
        move.start()
    moves[0].wait()
    moves[1].wait()
    shape, rate = bs_s[...], br_s[...]
    genes = shape.shape[0]
    gene_ref[:genes] = jnp.exp(digamma_series(shape) - jnp.log(rate)).astype(BF16)
    beta = jnp.sum(shape / rate, axis=0, keepdims=True)
    moves[2].wait()
    moves[3].wait()
    shape, rate = ts_s[...], tr_s[...]
    weight = jnp.exp(digamma_series(shape) - jnp.log(rate)).astype(BF16)
    for copy in range(cell_ref.shape[0]):
        cell_ref[copy] = weight
    gene_ref[genes:] = split_rows(beta, jnp.sum(shape / rate, axis=0, keepdims=True))


def weights_call(theta_shape, theta_rate, beta_shape, beta_rate):
    cells, width = theta_shape.shape
    genes = beta_shape.shape[0]
    return pl.pallas_call(
        weights_kernel,
        in_specs=[HBM] * 4,
        out_specs=[VMEM] * 2,
        out_shape=[
            jax.ShapeDtypeStruct((8, cells, width), BF16),
            jax.ShapeDtypeStruct((genes + EXTRA, width), BF16),
        ],
        scratch_shapes=[pltpu.VMEM((cells, width), F32)] * 2
        + [pltpu.VMEM((genes, width), F32)] * 2
        + [pltpu.SemaphoreType.DMA((4,))],
        compiler_params=pltpu.CompilerParams(vmem_limit_bytes=55152 * 1024),
    )(theta_shape, theta_rate, beta_shape, beta_rate)


def main_kernel(
    ids_ref, live_ref, cell_ref, own_ref, oth_ref, counts_ref,
    cell_out, keep_out, send_out,
    ids_s, live_s, counts_s, rows_s, cols_s, acc_s, gene_s, sems, id_sem, live_sem,
):
    parts, part, width = cell_ref.shape
    block = own_ref.shape[1] - EXTRA
    sides = own_ref.shape[0]
    cells = parts * part
    groups = counts_ref.shape[0] // GROUP
    my_y, my_x, my_core = lax.axis_index("y"), lax.axis_index("x"), lax.axis_index("core")

    def fetch(group):
        here = pl.ds(group * GROUP, GROUP)
        return pltpu.make_async_copy(counts_ref.at[here], counts_s.at[here], sems.at[group])

    live_copy = pltpu.make_async_copy(live_ref, live_s, live_sem)
    ids_copy = pltpu.make_async_copy(ids_ref, ids_s, id_sem)
    live_copy.start()
    ids_copy.start()
    fetch(0).start()
    for index in range(parts):
        rows = cell_ref[index]
        rows_s[pl.ds(index * part, part), :] = rows
        cols_s[:, pl.ds(index * part, part)] = rows.T
    gene_s[...] = jnp.zeros_like(gene_s)
    live_copy.wait()
    ids_copy.wait()
    live = live_s[0, 0]
    for group in range(1, groups):
        @pl.when(GROUP * group < live)
        def _():
            fetch(group).start()

    def place(slot):
        index = ids_s[0, 0, slot]
        core, x, y = index % 2, (index // 2) % 4, index // 8
        from_x, from_y = (my_x - x + 4) % 4, (my_y - y + 4) % 4
        spot = jnp.where(core == 0, from_y * 4 + from_x, from_x * 4 + from_y)
        return index, core == my_core, spot

    def block_of(slot):
        _, mine, spot = place(slot)
        return jnp.where(mine, own_ref[spot, :block], oth_ref[spot, :block])

    for group in range(groups):
        @pl.when(GROUP * group < live)
        def _():
            slots = [GROUP * group + index for index in range(GROUP)]
            alive = [slot < live for slot in slots]
            pair = jnp.concatenate([block_of(slot) for slot in slots], axis=0)
            fetch(group).wait()
            total = jnp.zeros((width, GROUP * block), F32)
            for start in range(0, cells, CHUNK):
                here = pl.ds(start, CHUNK)
                rate = lax.dot_general(
                    rows_s[here, :], pair, (((1,), (1,)), ((), ())), preferred_element_type=F32
                )
                ratios = []
                for index in range(GROUP):
                    columns = slice(index * block, (index + 1) * block)
                    ratio = counts_s[slots[index], here, :].astype(F32) / rate[:, columns]
                    if slots[index] > 1:
                        ratio = jnp.where(alive[index], ratio, 0.0)
                    ratios.append(ratio.astype(BF16))
                ratio = jnp.concatenate(ratios, axis=1)
                term = jnp.dot(ratio, pair, preferred_element_type=F32)
                if group == 0:
                    acc_s[here, :] = term
                else:
                    acc_s[here, :] += term
                total += jnp.dot(cols_s[:, here], ratio, preferred_element_type=F32)
            total = total.T
            for k in range(GROUP):
                @pl.when(alive[k])
                def _():
                    index, mine, _ = place(slots[k])
                    gene_s[jnp.where(mine, 0, 1), index // 2] = total[k * block : (k + 1) * block]

    totals = row_totals(jnp.concatenate([own_ref[:, block:], oth_ref[:, block:]], axis=0))
    extra = split_rows(*totals)
    for index in range(parts):
        cell_out[index, :part] = acc_s[pl.ds(index * part, part), :].astype(BF16)
        cell_out[index, part:] = extra
    for index in range(sides):
        keep_out[index] = gene_s[0, index]
        send_out[index] = gene_s[1, index].astype(BF16)


def main_call(ids, live, cell_rows, own, other, counts):
    slots, cells, block = counts.shape
    parts, part, width = cell_rows.shape
    sides = own.shape[0]
    return pl.pallas_call(
        main_kernel,
        in_specs=[HBM, HBM, VMEM, VMEM, VMEM, HBM],
        out_specs=[VMEM, VMEM, VMEM],
        scratch_shapes=[
            pltpu.SMEM(ids.shape, jnp.int32),
            pltpu.SMEM(live.shape, jnp.int32),
            pltpu.VMEM((slots, cells, block), BF16),
            pltpu.VMEM((cells, width), BF16),
            pltpu.VMEM((width, cells), BF16),
            pltpu.VMEM((cells, width), F32),
            pltpu.VMEM((2, sides, block, width), F32),
            pltpu.SemaphoreType.DMA((slots // GROUP,)),
            pltpu.SemaphoreType.DMA,
            pltpu.SemaphoreType.DMA,
        ],
        out_shape=[
            jax.ShapeDtypeStruct((parts, part + EXTRA, width), BF16),
            jax.ShapeDtypeStruct((sides, block, width), F32),
            jax.ShapeDtypeStruct((sides, block, width), BF16),
        ],
        compiler_params=params(48),
    )(ids, live, cell_rows, own, other, counts)


def first_and_second():
    my_y, my_x, core = lax.axis_index("y"), lax.axis_index("x"), lax.axis_index("core")
    return core, jnp.where(core == 0, my_x, my_y), jnp.where(core == 0, my_y, my_x)


def core_sum_kernel(keep_ref, got_ref, mine_ref, *send_refs):
    core, first, _ = first_and_second()
    for row in range(4):
        for step in range(4):
            along = (first + step) % 4
            spot = jnp.where(core == 0, row * 4 + along, along * 4 + row)
            value = keep_ref[spot] + got_ref[spot].astype(F32)
            if step == 0:
                mine_ref[row] = value
            else:
                send_refs[step - 1][row] = value.astype(BF16)


def first_sum_kernel(keep_ref, a_ref, b_ref, c_ref, mine_ref, *send_refs):
    _, _, second = first_and_second()
    for step in range(4):
        spot = (second + step) % 4
        value = keep_ref[spot] + a_ref[spot].astype(F32)
        value += b_ref[spot].astype(F32) + c_ref[spot].astype(F32)
        if step == 0:
            mine_ref[...] = value
        else:
            send_refs[step - 1][...] = value.astype(BF16)


def finish(weight, stat, activity, total, shape_ref, rate_ref):
    rows, width = stat.shape
    shape_ref[...] = jnp.log(0.3 + weight.astype(F32) * stat)
    for start in range(0, rows, 128):
        here = pl.ds(start, 128)
        column = jnp.broadcast_to(activity[:, start : start + 128], (width, 128)).T
        rate_ref[here, :] = jnp.log(column + total)


def gene_finish_kernel(keep_ref, a_ref, b_ref, c_ref, got_ref, weight_ref, act_ref, shape_ref, rate_ref):
    value = keep_ref[...] + a_ref[...].astype(F32)
    value += b_ref[...].astype(F32) + c_ref[...].astype(F32)
    rows = value.shape[0]
    _, theta = row_totals(got_ref[:, got_ref.shape[1] - EXTRA :])
    finish(weight_ref[:rows], value, act_ref[...], theta, shape_ref, rate_ref)


def cell_finish_kernel(got_ref, weights_ref, act_ref, shape_ref, rate_ref):
    parts, rows, _ = weights_ref.shape
    value = got_ref[0, :rows].astype(F32)
    for index in range(1, parts):
        value += got_ref[index, :rows].astype(F32)
    beta, _ = row_totals(got_ref[:, rows:])
    finish(weights_ref[lax.axis_index("z")], value, act_ref[...], beta, shape_ref, rate_ref)


def simple_call(kernel, out_shape, *args, mib=16):
    return pl.pallas_call(
        kernel,
        in_specs=[VMEM] * len(args),
        out_specs=[VMEM] * len(out_shape),
        out_shape=out_shape,
        compiler_params=params(mib),
    )(*args)


def shift(stage, step, value):
    pairs = []
    for y in range(4):
        for x in range(4):
            for core in range(2):
                if core == stage:
                    to_y, to_x = y, (x + step) % 4
                else:
                    to_y, to_x = (y + step) % 4, x
                pairs.append(((y * 4 + x) * 2 + core, (to_y * 4 + to_x) * 2 + core))
    return lax.ppermute(value, ("y", "x", "core"), pairs)


def swap_cores(value):
    return lax.ppermute(value, "core", [(0, 1), (1, 0)])


def on_device(
    theta_shape,
    theta_rate,
    cell_activity,
    beta_shape,
    beta_rate,
    gene_activity,
    block_ids,
    live_blocks,
    counts,
):
    cells, width = theta_shape.shape
    genes = beta_shape.shape[0]
    struct = jax.ShapeDtypeStruct
    steps = (1, 2, 3)
    cell_pay, gene_pay = weights_call(theta_shape, theta_rate, beta_shape, beta_rate)
    cell_rows = lax.all_to_all(cell_pay, "z", 0, 0)
    got = {step: shift(0, step, gene_pay) for step in steps}
    line = jnp.stack([gene_pay, got[1], got[2], got[3]])
    got = {step: shift(1, step, line) for step in steps}
    ids = jnp.maximum(block_ids, 0)
    got, ids = lax.optimization_barrier((got, ids))
    own = jnp.concatenate([line, got[1], got[2], got[3]])
    other = swap_cores(own)

    cell_part, keep, send = main_call(ids, live_blocks, cell_rows, own, other, counts[0])
    cell_got = lax.all_to_all(cell_part, "z", 0, 0)
    keep, *sends = simple_call(
        core_sum_kernel,
        [struct((4, genes, width), F32)] + [struct((4, genes, width), BF16)] * 3,
        keep, swap_cores(send),
    )
    gots = [shift(0, step, sends[step - 1]) for step in steps]
    keep, *sends = simple_call(
        first_sum_kernel,
        [struct((genes, width), F32)] + [struct((genes, width), BF16)] * 3,
        keep, *gots,
    )
    gots = [shift(1, step, sends[step - 1]) for step in steps]
    log_theta = simple_call(
        cell_finish_kernel, [struct((cells, width), F32)] * 2,
        cell_got, cell_rows, cell_activity.reshape(1, cells),
    )
    gots, log_theta = lax.optimization_barrier((gots, log_theta))
    log_beta = simple_call(
        gene_finish_kernel, [struct((genes, width), F32)] * 2,
        keep, *gots, cell_got, gene_pay, gene_activity.reshape(1, genes),
    )
    return (*log_theta, *log_beta)


def solution(mesh):
    fine = Mesh(mesh.devices.reshape(4, 4, 2, 8), ("y", "x", "core", "z"))
    cells = ("y", "x", "core")
    every = cells + ("z",)
    in_specs = (
        P(every, None),
        P(every, None),
        P(every),
        P(every, None),
        P(every, None),
        P(every),
        P("z", cells, None),
        P("z", cells),
        P("z", None, cells, None),
    )
    out_specs = (P(every, None),) * 4
    return jax.shard_map(
        on_device, mesh=fine, in_specs=in_specs, out_specs=out_specs, check_vma=False
    )
```

```python
import jax
import jax.numpy as jnp
from jax import lax
from jax.experimental import pallas as pl
from jax.experimental.pallas import tpu as pltpu
from jax.sharding import Mesh, PartitionSpec as P

F32 = jnp.float32
BF16 = jnp.bfloat16
VMEM = pl.BlockSpec(memory_space=pltpu.VMEM)
HBM = pl.BlockSpec(memory_space=pltpu.HBM)
EXTRA = 16
CHUNK = 1024
GROUP = 4


def params(mib):
    return pltpu.CompilerParams(vmem_limit_bytes=mib * 1024 * 1024)


def digamma_series(value):
    shifted = value
    correction = jnp.zeros_like(value)
    for offset in range(6):
        correction = correction + 1.0 / shifted
        shifted = shifted + 1.0
    inverse = 1.0 / shifted
    square = inverse * inverse
    series = (
        jnp.log(shifted)
        - 0.5 * inverse
        - square * (1.0 / 12.0 - square * (1.0 / 120.0 - square * (1.0 / 252.0)))
    )
    return series - correction


def split_rows(beta, theta):
    row = lax.broadcasted_iota(jnp.int32, (EXTRA, beta.shape[1]), 0)
    block = jnp.zeros(row.shape, F32)
    for start, total in ((0, beta), (3, theta)):
        high = total.astype(BF16).astype(F32)
        middle = (total - high).astype(BF16).astype(F32)
        for index, part in enumerate((high, middle, total - high - middle)):
            block = jnp.where(row == start + index, part, block)
    return block.astype(BF16)


def row_totals(blocks):
    block = jnp.sum(blocks.astype(F32), axis=0)
    return jnp.sum(block[:3], axis=0, keepdims=True), jnp.sum(block[3:6], axis=0, keepdims=True)


def weights_kernel(ts_hbm, tr_hbm, bs_hbm, br_hbm, cell_ref, gene_ref, ts_s, tr_s, bs_s, br_s, sems):
    pairs = ((bs_hbm, bs_s), (br_hbm, br_s), (ts_hbm, ts_s), (tr_hbm, tr_s))
    moves = [pltpu.make_async_copy(*pair, sems.at[index]) for index, pair in enumerate(pairs)]
    for move in moves:
        move.start()
    moves[0].wait()
    moves[1].wait()
    shape, rate = bs_s[...], br_s[...]
    genes = shape.shape[0]
    gene_ref[:genes] = jnp.exp(digamma_series(shape) - jnp.log(rate)).astype(BF16)
    beta = jnp.sum(shape / rate, axis=0, keepdims=True)
    moves[2].wait()
    moves[3].wait()
    shape, rate = ts_s[...], tr_s[...]
    weight = jnp.exp(digamma_series(shape) - jnp.log(rate)).astype(BF16)
    for copy in range(cell_ref.shape[0]):
        cell_ref[copy] = weight
    gene_ref[genes:] = split_rows(beta, jnp.sum(shape / rate, axis=0, keepdims=True))


def weights_call(theta_shape, theta_rate, beta_shape, beta_rate):
    cells, width = theta_shape.shape
    genes = beta_shape.shape[0]
    return pl.pallas_call(
        weights_kernel,
        in_specs=[HBM] * 4,
        out_specs=[VMEM] * 2,
        out_shape=[
            jax.ShapeDtypeStruct((8, cells, width), BF16),
            jax.ShapeDtypeStruct((genes + EXTRA, width), BF16),
        ],
        scratch_shapes=[pltpu.VMEM((cells, width), F32)] * 2
        + [pltpu.VMEM((genes, width), F32)] * 2
        + [pltpu.SemaphoreType.DMA((4,))],
        compiler_params=pltpu.CompilerParams(vmem_limit_bytes=55152 * 1024),
    )(theta_shape, theta_rate, beta_shape, beta_rate)


def main_kernel(
    ids_ref, live_ref, cell_ref, own_ref, oth_ref, counts_ref,
    cell_out, keep_out, send_out,
    ids_s, live_s, counts_s, rows_s, cols_s, acc_s, gene_s, sems, id_sem, live_sem,
):
    parts, part, width = cell_ref.shape
    block = own_ref.shape[1] - EXTRA
    sides = own_ref.shape[0]
    cells = parts * part
    groups = counts_ref.shape[0] // GROUP
    my_y, my_x, my_core = lax.axis_index("y"), lax.axis_index("x"), lax.axis_index("core")

    def fetch(group):
        here = pl.ds(group * GROUP, GROUP)
        return pltpu.make_async_copy(counts_ref.at[here], counts_s.at[here], sems.at[group])

    live_copy = pltpu.make_async_copy(live_ref, live_s, live_sem)
    ids_copy = pltpu.make_async_copy(ids_ref, ids_s, id_sem)
    live_copy.start()
    ids_copy.start()
    fetch(0).start()
    for index in range(parts):
        rows = cell_ref[index]
        rows_s[pl.ds(pl.multiple_of(spot_of(index) * part, part), part), :] = rows
        cols_s[:, pl.ds(pl.multiple_of(spot_of(index) * part, part), part)] = rows.T
    gene_s[...] = jnp.zeros_like(gene_s)
    live_copy.wait()
    ids_copy.wait()
    live = live_s[0, 0]
    for group in range(1, groups):
        @pl.when(GROUP * group < live)
        def _():
            fetch(group).start()

    def place(slot):
        index = ids_s[0, 0, slot]
        core, x, y = index % 2, (index // 2) % 4, index // 8
        from_x, from_y = (my_x - x + 4) % 4, (my_y - y + 4) % 4
        spot = jnp.where(core == 0, from_y * 4 + from_x, from_x * 4 + from_y)
        return index, core == my_core, spot

    def block_of(slot):
        _, mine, spot = place(slot)
        return jnp.where(mine, own_ref[spot, :block], oth_ref[spot, :block])

    for group in range(groups):
        @pl.when(GROUP * group < live)
        def _():
            slots = [GROUP * group + index for index in range(GROUP)]
            alive = [slot < live for slot in slots]
            pair = jnp.concatenate([block_of(slot) for slot in slots], axis=0)
            fetch(group).wait()
            total = jnp.zeros((width, GROUP * block), F32)
            for start in range(0, cells, CHUNK):
                here = pl.ds(start, CHUNK)
                rate = lax.dot_general(
                    rows_s[here, :], pair, (((1,), (1,)), ((), ())), preferred_element_type=F32
                )
                ratios = []
                for index in range(GROUP):
                    columns = slice(index * block, (index + 1) * block)
                    ratio = counts_s[slots[index], here, :].astype(F32) / rate[:, columns]
                    if slots[index] > 1:
                        ratio = jnp.where(alive[index], ratio, 0.0)
                    ratios.append(ratio.astype(BF16))
                ratio = jnp.concatenate(ratios, axis=1)
                term = jnp.dot(ratio, pair, preferred_element_type=F32)
                if group == 0:
                    acc_s[here, :] = term
                else:
                    acc_s[here, :] += term
                total += jnp.dot(cols_s[:, here], ratio, preferred_element_type=F32)
            total = total.T
            for k in range(GROUP):
                @pl.when(alive[k])
                def _():
                    index, mine, _ = place(slots[k])
                    gene_s[jnp.where(mine, 0, 1), index // 2] = total[k * block : (k + 1) * block]

    totals = row_totals(jnp.concatenate([own_ref[:, block:], oth_ref[:, block:]], axis=0))
    extra = split_rows(*totals)
    for index in range(parts):
        cell_out[index, :part] = acc_s[pl.ds(pl.multiple_of(spot_of(index) * part, part), part), :].astype(BF16)
        cell_out[index, part:] = extra
    for index in range(sides):
        keep_out[index] = gene_s[0, index]
        send_out[index] = gene_s[1, index].astype(BF16)


def main_call(ids, live, cell_rows, own, other, counts):
    slots, cells, block = counts.shape
    parts, part, width = cell_rows.shape
    sides = own.shape[0]
    return pl.pallas_call(
        main_kernel,
        in_specs=[HBM, HBM, VMEM, VMEM, VMEM, HBM],
        out_specs=[VMEM, VMEM, VMEM],
        scratch_shapes=[
            pltpu.SMEM(ids.shape, jnp.int32),
            pltpu.SMEM(live.shape, jnp.int32),
            pltpu.VMEM((slots, cells, block), BF16),
            pltpu.VMEM((cells, width), BF16),
            pltpu.VMEM((width, cells), BF16),
            pltpu.VMEM((cells, width), F32),
            pltpu.VMEM((2, sides, block, width), F32),
            pltpu.SemaphoreType.DMA((slots // GROUP,)),
            pltpu.SemaphoreType.DMA,
            pltpu.SemaphoreType.DMA,
        ],
        out_shape=[
            jax.ShapeDtypeStruct((parts, part + EXTRA, width), BF16),
            jax.ShapeDtypeStruct((sides, block, width), F32),
            jax.ShapeDtypeStruct((sides, block, width), BF16),
        ],
        compiler_params=params(48),
    )(ids, live, cell_rows, own, other, counts)


def first_and_second():
    my_y, my_x, core = lax.axis_index("y"), lax.axis_index("x"), lax.axis_index("core")
    return core, jnp.where(core == 0, my_x, my_y), jnp.where(core == 0, my_y, my_x)


def core_sum_kernel(keep_ref, got_ref, mine_ref, *send_refs):
    core, first, _ = first_and_second()
    for row in range(4):
        for step in range(4):
            along = (first + step) % 4
            spot = jnp.where(core == 0, row * 4 + along, along * 4 + row)
            value = keep_ref[spot] + got_ref[spot].astype(F32)
            if step == 0:
                mine_ref[row] = value
            else:
                send_refs[step - 1][row] = value.astype(BF16)


def first_sum_kernel(keep_ref, a_ref, b_ref, c_ref, mine_ref, *send_refs):
    _, _, second = first_and_second()
    for step in range(4):
        spot = (second + step) % 4
        value = keep_ref[spot] + a_ref[spot].astype(F32)
        value += b_ref[spot].astype(F32) + c_ref[spot].astype(F32)
        if step == 0:
            mine_ref[...] = value
        else:
            send_refs[step - 1][...] = value.astype(BF16)


def finish(weight, stat, activity, total, shape_ref, rate_ref):
    rows, width = stat.shape
    shape_ref[...] = jnp.log(0.3 + weight.astype(F32) * stat)
    for start in range(0, rows, 128):
        here = pl.ds(start, 128)
        column = jnp.broadcast_to(activity[:, start : start + 128], (width, 128)).T
        rate_ref[here, :] = jnp.log(column + total)


def gene_finish_kernel(keep_ref, a_ref, b_ref, c_ref, got_ref, weight_ref, act_ref, shape_ref, rate_ref):
    value = keep_ref[...] + a_ref[...].astype(F32)
    value += b_ref[...].astype(F32) + c_ref[...].astype(F32)
    rows = value.shape[0]
    _, theta = row_totals(got_ref[:, got_ref.shape[1] - EXTRA :])
    finish(weight_ref[:rows], value, act_ref[...], theta, shape_ref, rate_ref)


def cell_finish_kernel(got_ref, weights_ref, act_ref, shape_ref, rate_ref):
    parts, rows, _ = weights_ref.shape
    value = got_ref[0, :rows].astype(F32)
    for index in range(1, parts):
        value += got_ref[index, :rows].astype(F32)
    beta, _ = row_totals(got_ref[:, rows:])
    finish(weights_ref[spot_of(lax.axis_index("z"))], value, act_ref[...], beta, shape_ref, rate_ref)


def spot_of(index):
    return jnp.where(lax.axis_index("core") == 0, index, 7 - index)


def exchange(value):
    groups = [list(range(8)), [8 + 7 - index for index in range(8)]]
    return lax.all_to_all(value, ("core", "z"), 0, 0, axis_index_groups=groups)


def simple_call(kernel, out_shape, *args, mib=16):
    return pl.pallas_call(
        kernel,
        in_specs=[VMEM] * len(args),
        out_specs=[VMEM] * len(out_shape),
        out_shape=out_shape,
        compiler_params=params(mib),
    )(*args)


def shift(stage, step, value):
    pairs = []
    for y in range(4):
        for x in range(4):
            for core in range(2):
                if core == stage:
                    to_y, to_x = y, (x + step) % 4
                else:
                    to_y, to_x = (y + step) % 4, x
                pairs.append(((y * 4 + x) * 2 + core, (to_y * 4 + to_x) * 2 + core))
    return lax.ppermute(value, ("y", "x", "core"), pairs)


def swap_cores(value):
    return lax.ppermute(value, "core", [(0, 1), (1, 0)])


def on_device(
    theta_shape,
    theta_rate,
    cell_activity,
    beta_shape,
    beta_rate,
    gene_activity,
    block_ids,
    live_blocks,
    counts,
):
    cells, width = theta_shape.shape
    genes = beta_shape.shape[0]
    struct = jax.ShapeDtypeStruct
    steps = (1, 2, 3)
    cell_pay, gene_pay = weights_call(theta_shape, theta_rate, beta_shape, beta_rate)
    cell_rows = exchange(cell_pay)
    got = {step: shift(0, step, gene_pay) for step in steps}
    line = jnp.stack([gene_pay, got[1], got[2], got[3]])
    got = {step: shift(1, step, line) for step in steps}
    ids = jnp.maximum(block_ids, 0)
    got, ids = lax.optimization_barrier((got, ids))
    own = jnp.concatenate([line, got[1], got[2], got[3]])
    other = swap_cores(own)

    cell_part, keep, send = main_call(ids, live_blocks, cell_rows, own, other, counts[0])
    cell_got = exchange(cell_part)
    keep, *sends = simple_call(
        core_sum_kernel,
        [struct((4, genes, width), F32)] + [struct((4, genes, width), BF16)] * 3,
        keep, swap_cores(send),
    )
    gots = [shift(0, step, sends[step - 1]) for step in steps]
    keep, *sends = simple_call(
        first_sum_kernel,
        [struct((genes, width), F32)] + [struct((genes, width), BF16)] * 3,
        keep, *gots,
    )
    gots = [shift(1, step, sends[step - 1]) for step in steps]
    log_theta = simple_call(
        cell_finish_kernel, [struct((cells, width), F32)] * 2,
        cell_got, cell_rows, cell_activity.reshape(1, cells),
    )
    gots, log_theta = lax.optimization_barrier((gots, log_theta))
    log_beta = simple_call(
        gene_finish_kernel, [struct((genes, width), F32)] * 2,
        keep, *gots, cell_got, gene_pay, gene_activity.reshape(1, genes),
    )
    return (*log_theta, *log_beta)


def solution(mesh):
    fine = Mesh(mesh.devices.reshape(4, 4, 2, 8), ("y", "x", "core", "z"))
    cells = ("y", "x", "core")
    every = cells + ("z",)
    in_specs = (
        P(every, None),
        P(every, None),
        P(every),
        P(every, None),
        P(every, None),
        P(every),
        P("z", cells, None),
        P("z", cells),
        P("z", None, cells, None),
    )
    out_specs = (P(every, None),) * 4
    return jax.shard_map(
        on_device, mesh=fine, in_specs=in_specs, out_specs=out_specs, check_vma=False
    )
```

```python
import jax
import jax.numpy as jnp
from jax import lax
from jax.experimental import pallas as pl
from jax.experimental.pallas import tpu as pltpu
from jax.sharding import Mesh, PartitionSpec as P

F32 = jnp.float32
BF16 = jnp.bfloat16
VMEM = pl.BlockSpec(memory_space=pltpu.VMEM)
HBM = pl.BlockSpec(memory_space=pltpu.HBM)
EXTRA = 16
CHUNK = 1024
GROUP = 4


def params(mib):
    return pltpu.CompilerParams(vmem_limit_bytes=mib * 1024 * 1024)


def digamma_series(value):
    shifted = value
    correction = jnp.zeros_like(value)
    for offset in range(6):
        correction = correction + 1.0 / shifted
        shifted = shifted + 1.0
    inverse = 1.0 / shifted
    square = inverse * inverse
    series = (
        jnp.log(shifted)
        - 0.5 * inverse
        - square * (1.0 / 12.0 - square * (1.0 / 120.0 - square * (1.0 / 252.0)))
    )
    return series - correction


def split_rows(beta, theta):
    row = lax.broadcasted_iota(jnp.int32, (EXTRA, beta.shape[1]), 0)
    block = jnp.zeros(row.shape, F32)
    for start, total in ((0, beta), (3, theta)):
        high = total.astype(BF16).astype(F32)
        middle = (total - high).astype(BF16).astype(F32)
        for index, part in enumerate((high, middle, total - high - middle)):
            block = jnp.where(row == start + index, part, block)
    return block.astype(BF16)


def row_totals(blocks):
    block = jnp.sum(blocks.astype(F32), axis=0)
    return jnp.sum(block[:3], axis=0, keepdims=True), jnp.sum(block[3:6], axis=0, keepdims=True)


def weights_kernel(ts_hbm, tr_hbm, bs_hbm, br_hbm, cell_ref, gene_ref, ts_s, tr_s, bs_s, br_s, sems):
    pairs = ((bs_hbm, bs_s), (br_hbm, br_s), (ts_hbm, ts_s), (tr_hbm, tr_s))
    moves = [pltpu.make_async_copy(*pair, sems.at[index]) for index, pair in enumerate(pairs)]
    for move in moves:
        move.start()
    moves[0].wait()
    moves[1].wait()
    shape, rate = bs_s[...], br_s[...]
    genes = shape.shape[0]
    gene_ref[:genes] = jnp.exp(digamma_series(shape) - jnp.log(rate)).astype(BF16)
    beta = jnp.sum(shape / rate, axis=0, keepdims=True)
    moves[2].wait()
    moves[3].wait()
    shape, rate = ts_s[...], tr_s[...]
    weight = jnp.exp(digamma_series(shape) - jnp.log(rate)).astype(BF16)
    for copy in range(cell_ref.shape[0]):
        cell_ref[copy] = weight
    gene_ref[genes:] = split_rows(beta, jnp.sum(shape / rate, axis=0, keepdims=True))


def weights_call(theta_shape, theta_rate, beta_shape, beta_rate):
    cells, width = theta_shape.shape
    genes = beta_shape.shape[0]
    return pl.pallas_call(
        weights_kernel,
        in_specs=[HBM] * 4,
        out_specs=[VMEM] * 2,
        out_shape=[
            jax.ShapeDtypeStruct((8, cells, width), BF16),
            jax.ShapeDtypeStruct((genes + EXTRA, width), BF16),
        ],
        scratch_shapes=[pltpu.VMEM((cells, width), F32)] * 2
        + [pltpu.VMEM((genes, width), F32)] * 2
        + [pltpu.SemaphoreType.DMA((4,))],
        compiler_params=pltpu.CompilerParams(vmem_limit_bytes=55152 * 1024),
    )(theta_shape, theta_rate, beta_shape, beta_rate)


def main_kernel(
    ids_ref, live_ref, cell_ref, own_ref, oth_ref, counts_ref,
    cell_out, keep_out, send_out,
    ids_s, live_s, counts_s, rows_s, cols_s, acc_s, gene_s, sems, id_sem, live_sem,
):
    parts, part, width = cell_ref.shape
    block = own_ref.shape[1] - EXTRA
    sides = own_ref.shape[0]
    cells = parts * part
    groups = counts_ref.shape[0] // GROUP
    my_y, my_x, my_core = lax.axis_index("y"), lax.axis_index("x"), lax.axis_index("core")

    def fetch(group):
        here = pl.ds(group * GROUP, GROUP)
        return pltpu.make_async_copy(counts_ref.at[here], counts_s.at[here], sems.at[group])

    live_copy = pltpu.make_async_copy(live_ref, live_s, live_sem)
    ids_copy = pltpu.make_async_copy(ids_ref, ids_s, id_sem)
    live_copy.start()
    ids_copy.start()
    fetch(0).start()
    for index in range(parts):
        rows = cell_ref[index]
        rows_s[pl.ds(pl.multiple_of(spot_of(index) * part, part), part), :] = rows
        cols_s[:, pl.ds(pl.multiple_of(spot_of(index) * part, part), part)] = rows.T
    gene_s[...] = jnp.zeros_like(gene_s)
    live_copy.wait()
    ids_copy.wait()
    live = live_s[0, 0]
    for group in range(1, groups):
        @pl.when(GROUP * group < live)
        def _():
            fetch(group).start()

    def place(slot):
        index = ids_s[0, 0, slot]
        core, x, y = index % 2, (index // 2) % 4, index // 8
        from_x, from_y = (my_x - x + 4) % 4, (my_y - y + 4) % 4
        spot = jnp.where(core == 0, from_y * 4 + from_x, from_x * 4 + from_y)
        return index, core == my_core, spot

    def block_of(slot):
        _, mine, spot = place(slot)
        return jnp.where(mine, own_ref[spot, :block], oth_ref[spot, :block])

    for group in range(groups):
        @pl.when(GROUP * group < live)
        def _():
            slots = [GROUP * group + index for index in range(GROUP)]
            alive = [slot < live for slot in slots]
            pair = jnp.concatenate([block_of(slot) for slot in slots], axis=0)
            fetch(group).wait()
            total = jnp.zeros((width, GROUP * block), F32)
            for start in range(0, cells, CHUNK):
                here = pl.ds(start, CHUNK)
                rate = lax.dot_general(
                    rows_s[here, :], pair, (((1,), (1,)), ((), ())), preferred_element_type=F32
                )
                ratios = []
                for index in range(GROUP):
                    columns = slice(index * block, (index + 1) * block)
                    ratio = counts_s[slots[index], here, :].astype(F32) / rate[:, columns]
                    if slots[index] > 1:
                        ratio = jnp.where(alive[index], ratio, 0.0)
                    ratios.append(ratio.astype(BF16))
                ratio = jnp.concatenate(ratios, axis=1)
                term = jnp.dot(ratio, pair, preferred_element_type=F32)
                if group == 0:
                    acc_s[here, :] = term
                else:
                    acc_s[here, :] += term
                total += jnp.dot(cols_s[:, here], ratio, preferred_element_type=F32)
            total = total.T
            for k in range(GROUP):
                @pl.when(alive[k])
                def _():
                    index, mine, _ = place(slots[k])
                    gene_s[jnp.where(mine, 0, 1), index // 2] = total[k * block : (k + 1) * block]

    totals = row_totals(jnp.concatenate([own_ref[:, block:], oth_ref[:, block:]], axis=0))
    extra = split_rows(*totals)
    for index in range(parts):
        cell_out[index, :part] = acc_s[pl.ds(pl.multiple_of(spot_of(index) * part, part), part), :].astype(BF16)
        cell_out[index, part:] = extra
    for index in range(sides):
        keep_out[index] = gene_s[0, index]
        send_out[index] = gene_s[1, index].astype(BF16)


def main_call(ids, live, cell_rows, own, other, counts):
    slots, cells, block = counts.shape
    parts, part, width = cell_rows.shape
    sides = own.shape[0]
    return pl.pallas_call(
        main_kernel,
        in_specs=[HBM, HBM, VMEM, VMEM, VMEM, HBM],
        out_specs=[VMEM, VMEM, VMEM],
        scratch_shapes=[
            pltpu.SMEM(ids.shape, jnp.int32),
            pltpu.SMEM(live.shape, jnp.int32),
            pltpu.VMEM((slots, cells, block), BF16),
            pltpu.VMEM((cells, width), BF16),
            pltpu.VMEM((width, cells), BF16),
            pltpu.VMEM((cells, width), F32),
            pltpu.VMEM((2, sides, block, width), F32),
            pltpu.SemaphoreType.DMA((slots // GROUP,)),
            pltpu.SemaphoreType.DMA,
            pltpu.SemaphoreType.DMA,
        ],
        out_shape=[
            jax.ShapeDtypeStruct((parts, part + EXTRA, width), BF16),
            jax.ShapeDtypeStruct((sides, block, width), F32),
            jax.ShapeDtypeStruct((sides, block, width), BF16),
        ],
        compiler_params=params(48),
    )(ids, live, cell_rows, own, other, counts)


def first_and_second():
    my_y, my_x, core = lax.axis_index("y"), lax.axis_index("x"), lax.axis_index("core")
    return core, jnp.where(core == 0, my_x, my_y), jnp.where(core == 0, my_y, my_x)


def core_sum_kernel(keep_ref, got_ref, mine_ref, *send_refs):
    core, first, _ = first_and_second()
    for row in range(4):
        for step in range(4):
            along = (first + step) % 4
            spot = jnp.where(core == 0, row * 4 + along, along * 4 + row)
            value = keep_ref[spot] + got_ref[spot].astype(F32)
            if step == 0:
                mine_ref[row] = value
            else:
                send_refs[step - 1][row] = value.astype(BF16)


def first_sum_kernel(keep_ref, a_ref, b_ref, c_ref, mine_ref, *send_refs):
    _, _, second = first_and_second()
    for step in range(4):
        spot = (second + step) % 4
        value = keep_ref[spot] + a_ref[spot].astype(F32)
        value += b_ref[spot].astype(F32) + c_ref[spot].astype(F32)
        if step == 0:
            mine_ref[...] = value
        else:
            send_refs[step - 1][...] = value.astype(BF16)


def finish(weight, stat, activity, total, shape_ref, rate_ref):
    rows, width = stat.shape
    shape_ref[...] = jnp.log(0.3 + weight.astype(F32) * stat)
    for start in range(0, rows, 128):
        here = pl.ds(start, 128)
        column = jnp.broadcast_to(activity[:, start : start + 128], (width, 128)).T
        rate_ref[here, :] = jnp.log(column + total)


def gene_finish_kernel(keep_ref, a_ref, b_ref, c_ref, got_ref, weight_ref, act_ref, shape_ref, rate_ref):
    value = keep_ref[...] + a_ref[...].astype(F32)
    value += b_ref[...].astype(F32) + c_ref[...].astype(F32)
    rows = value.shape[0]
    _, theta = row_totals(got_ref[:, got_ref.shape[1] - EXTRA :])
    finish(weight_ref[:rows], value, act_ref[...], theta, shape_ref, rate_ref)


def cell_finish_kernel(got_ref, weights_ref, act_ref, shape_ref, rate_ref):
    parts, rows, _ = weights_ref.shape
    value = got_ref[0, :rows].astype(F32)
    for index in range(1, parts):
        value += got_ref[index, :rows].astype(F32)
    beta, _ = row_totals(got_ref[:, rows:])
    finish(weights_ref[spot_of(lax.axis_index("z"))], value, act_ref[...], beta, shape_ref, rate_ref)


def spot_of(index):
    return jnp.where(lax.axis_index("core") == 0, index, 7 - index)


def exchange(value):
    groups = [list(range(8)), [8 + 7 - index for index in range(8)]]
    return lax.all_to_all(value, ("core", "z"), 0, 0, axis_index_groups=groups)


def simple_call(kernel, out_shape, *args, mib=16):
    return pl.pallas_call(
        kernel,
        in_specs=[VMEM] * len(args),
        out_specs=[VMEM] * len(out_shape),
        out_shape=out_shape,
        compiler_params=params(mib),
    )(*args)


def shift(stage, step, value):
    pairs = []
    for y in range(4):
        for x in range(4):
            for core in range(2):
                if core == stage:
                    to_y, to_x = y, (x + step) % 4
                else:
                    to_y, to_x = (y + step) % 4, x
                pairs.append(((y * 4 + x) * 2 + core, (to_y * 4 + to_x) * 2 + core))
    return lax.ppermute(value, ("y", "x", "core"), pairs)


def swap_cores(value):
    return lax.ppermute(value, "core", [(0, 1), (1, 0)])


def on_device(
    theta_shape,
    theta_rate,
    cell_activity,
    beta_shape,
    beta_rate,
    gene_activity,
    block_ids,
    live_blocks,
    counts,
):
    cells, width = theta_shape.shape
    genes = beta_shape.shape[0]
    struct = jax.ShapeDtypeStruct
    steps = (1, 2, 3)
    cell_pay, gene_pay = weights_call(theta_shape, theta_rate, beta_shape, beta_rate)
    cell_rows = exchange(cell_pay)
    got = {step: shift(0, step, gene_pay) for step in steps}
    line = jnp.stack([gene_pay, got[1], got[2], got[3]])
    got = {step: shift(1, step, line) for step in steps}
    got[1], ids = lax.optimization_barrier((got[1], block_ids))
    ids = jnp.maximum(ids, 0)
    own = jnp.concatenate([line, got[1], got[2], got[3]])
    other = swap_cores(own)

    cell_part, keep, send = main_call(ids, live_blocks, cell_rows, own, other, counts[0])
    cell_got = exchange(cell_part)
    keep, *sends = simple_call(
        core_sum_kernel,
        [struct((4, genes, width), F32)] + [struct((4, genes, width), BF16)] * 3,
        keep, swap_cores(send),
    )
    gots = [shift(0, step, sends[step - 1]) for step in steps]
    keep, *sends = simple_call(
        first_sum_kernel,
        [struct((genes, width), F32)] + [struct((genes, width), BF16)] * 3,
        keep, *gots,
    )
    gots = [shift(1, step, sends[step - 1]) for step in steps]
    log_theta = simple_call(
        cell_finish_kernel, [struct((cells, width), F32)] * 2,
        cell_got, cell_rows, cell_activity.reshape(1, cells),
    )
    gots, log_theta = lax.optimization_barrier((gots, log_theta))
    log_beta = simple_call(
        gene_finish_kernel, [struct((genes, width), F32)] * 2,
        keep, *gots, cell_got, gene_pay, gene_activity.reshape(1, genes),
    )
    return (*log_theta, *log_beta)


def solution(mesh):
    fine = Mesh(mesh.devices.reshape(4, 4, 2, 8), ("y", "x", "core", "z"))
    cells = ("y", "x", "core")
    every = cells + ("z",)
    in_specs = (
        P(every, None),
        P(every, None),
        P(every),
        P(every, None),
        P(every, None),
        P(every),
        P("z", cells, None),
        P("z", cells),
        P("z", None, cells, None),
    )
    out_specs = (P(every, None),) * 4
    return jax.shard_map(
        on_device, mesh=fine, in_specs=in_specs, out_specs=out_specs, check_vma=False
    )
```
